256 devices in a mesh: blk: 16 (over x_lo, y, core), dp: 16 (over x_hi, z).
Axes of the slice: x: 4 (x_hi: 2, x_lo: 2; x = x_hi * 2 + x_lo), y: 4, z: 8, core: 2. Of those that a mesh axis runs over, the one named last changes fastest.
Arguments:
- normed_input: bfloat16 [256, 256, 5120], P(('blk', 'dp')), may hold values from -40 to 40
- segment_ids: int32 [16, 16, 256], P('dp'), may hold values from 0 to 3, never falling along the last dimension, each value on 1 to 128 neighbouring positions
- weights_qkv: bfloat16 [16, 5120, 384], P('blk'), may hold values from -0.08385255 to 0.08385255
- weights_out: bfloat16 [16, 128, 5120], P('blk'), may hold values from -0.5 to 0.5
- cotangent: bfloat16 [256, 256, 5120], P(('blk', 'dp')), may hold values from -24 to 24
Outputs:
- input_grad: bfloat16 [256, 256, 5120], P(('blk', 'dp'))
- grad_qkv: bfloat16 [16, 5120, 384], P('blk', 'dp')
- grad_out: bfloat16 [16, 128, 5120], P('blk', None, 'dp')
The draws below stay inside these ranges and needn't reach their ends.
All inputs are finite; a program needn't handle non-finite values.
Results may differ from the reference program's by a relative error of at most 0.02.
Values may be sent and summed in bfloat16 or wider, within the bound.
No kernel may reach another device: no remote copies, remote signals or barrier semaphores. Data moves between devices by JAX's collectives and lax.ppermute only.
A program may use at most 128 MiB of HBM per device.

```python
import math
import jax
import jax.numpy as jnp
import numpy as np
from jax import lax

D = 5120
HD = 128
LEN = 256
GROUPS = 16
SEQS = 256
N_BLK = 16
N_DP = 16


def draw_normed_input(key, part):
    key = jax.random.fold_in(key, 11)
    first = jax.random.fold_in(key, 0)
    base = jax.random.normal(first, (SEQS, LEN, D), jnp.float32)
    return base.astype(jnp.bfloat16)


def draw_weights_qkv(key, part):
    key = jax.random.fold_in(key, 23)
    scale = D ** (-0.5)
    base = jnp.clip(jax.random.normal(key, (GROUPS, D, 3 * HD), jnp.float32), -5.0, 5.0)
    return (base * scale).astype(jnp.bfloat16)


def spiked(result, own_key, source, target, shards_of, factor):
    def block_of(position):
        return (jnp.arange(result.shape[position]) // (result.shape[position] // shards_of)).reshape((-1,) + (1,) * (result.ndim - 1 - position))

    near = jax.random.permutation(own_key, shards_of)[block_of(target)]
    other_side = (block_of(target) + shards_of // 2) % shards_of
    return jnp.where((block_of(source) == near) | (block_of(source) == other_side), factor * result, result)


def block_levels(key, shape, shards, least, high):
    level = 1.0
    for axis_at, parts in shards:
        heights = jax.random.uniform(jax.random.fold_in(jax.random.fold_in(key, 6), axis_at), (parts,), jnp.float32, least / len(shards), high / len(shards))
        level = level * jnp.repeat(jnp.exp(heights), shape[axis_at] // parts).reshape((-1,) + (1,) * (len(shape) - 1 - axis_at))
    return level


def profile(number_of, total, bound, lean):
    loads = [(1 << 20) // math.isqrt(rank ** lean) + 1 for rank in range(2, number_of + 1)]
    rest, given = total - bound - (number_of - 1), [1] * (number_of - 1)
    while rest > 0:
        candidates = [i for i in range(number_of - 1) if given[i] < bound]
        pool, budget = sum([loads[i] for i in candidates]), rest
        for i in candidates:
            more = min(bound - given[i], max(1, budget * loads[i] // pool), rest)
            given[i] = given[i] + more
            rest = rest - more
    return np.array([bound] + given)


def uneven(stream_key, number_of, total, limit, slope):
    if number_of == 2:
        one = jax.random.randint(stream_key, (), max(1, total - limit), min(limit, total - 1) + 1)
        return jnp.stack([one, total - one])
    sizes = jnp.asarray(profile(number_of, total, limit, slope), jnp.int32)
    twos = (number_of - 1) // 2
    donor, receiver = sizes[1:1 + 2 * twos:2], sizes[2:2 + 2 * twos:2]
    slack = jnp.minimum(donor - 1, limit - receiver)
    moved = jax.random.randint(jax.random.fold_in(stream_key, 1), (twos,), 0, 1 << 20) % (slack + 1)
    sizes = sizes.at[1:1 + 2 * twos:2].set(donor - moved).at[2:2 + 2 * twos:2].set(receiver + moved)
    return sizes[jax.random.permutation(jax.random.fold_in(stream_key, 2), number_of)]


def noise(own_key, shape, scale, most, cuts=(), kind=jnp.bfloat16):
    array = scale * jax.random.normal(own_key, shape, jnp.float32)
    if cuts:
        array = array * block_levels(own_key, shape, cuts, -0.22, 0.18)
    return jnp.clip(array, -most, most).astype(kind)


def noise_with(stream_key, shape, width, bound, cuts, heavy, held_as=jnp.bfloat16):
    entries = width * jax.random.normal(stream_key, shape, jnp.float32)
    if cuts:
        entries = entries * block_levels(stream_key, shape, cuts, -0.22, 0.18)
    return jnp.clip(spiked(entries, jax.random.fold_in(stream_key, 3), *heavy), -bound, bound).astype(held_as)


def setup_inputs(seed: int = 0) -> dict:
    seeds = jax.random.split(jax.random.key(seed), 6)
    return {
        "normed_input": draw_normed_input(jax.random.fold_in(seeds[5], 71), 0),
        "segment_ids": jax.vmap(lambda own: jnp.searchsorted(jnp.cumsum(uneven(own, 4, LEN, LEN // 2, 1)), jnp.arange(LEN), side="right"))(jax.random.split(seeds[1], N_DP * N_BLK)).reshape((N_DP, N_BLK, LEN)).astype(jnp.int32),
        "weights_qkv": draw_weights_qkv(jax.random.fold_in(seeds[5], 71), 0),
        "weights_out": noise(seeds[3], (GROUPS, HD, D), HD ** -0.5, 0.5, ((0, 16),)),
        "cotangent": noise_with(seeds[4], (SEQS, LEN, D), 1.0, 24.0, ((0, 256),), (0, 2, 256, 6.0)),
    }


def group_terms(inputs, seg_row, w_qkv, w_out, grad_in):
    head = w_out.shape[0]
    scale = head ** -0.5
    qkv = jnp.dot(inputs, w_qkv, preferred_element_type=jnp.float32).astype(jnp.bfloat16)
    query = qkv[:, :head]
    keys = qkv[:, head:2 * head]
    values = qkv[:, 2 * head:]
    count = inputs.shape[0]
    places = jnp.arange(count, dtype=jnp.int32)
    allowed = (places[:, None] >= places[None, :]) & (seg_row[:, None] == seg_row[None, :])
    scores = jnp.dot(query, keys.T, preferred_element_type=jnp.float32) * scale
    scores = jnp.where(allowed, scores, jnp.float32(-1e30))
    top = jnp.max(scores, axis=-1, keepdims=True)
    expo = jnp.where(allowed, jnp.exp(scores - top), jnp.float32(0.0))
    probs = expo / jnp.sum(expo, axis=-1, keepdims=True)
    probs_b = probs.astype(jnp.bfloat16)
    attended = jnp.dot(probs_b, values, preferred_element_type=jnp.float32).astype(jnp.bfloat16)
    grad_wout = jnp.dot(attended.T, grad_in, preferred_element_type=jnp.float32)
    d_att = jnp.dot(grad_in, w_out.T, preferred_element_type=jnp.float32).astype(jnp.bfloat16)
    d_probs = jnp.dot(d_att, values.T, preferred_element_type=jnp.float32)
    d_scores = (probs * (d_probs - jnp.sum(probs * d_probs, axis=-1, keepdims=True)) * scale).astype(jnp.bfloat16)
    d_query = jnp.dot(d_scores, keys, preferred_element_type=jnp.float32)
    d_keys = jnp.dot(d_scores.T, query, preferred_element_type=jnp.float32)
    d_values = jnp.dot(probs_b.T, d_att, preferred_element_type=jnp.float32)
    d_qkv = jnp.concatenate([d_query, d_keys, d_values], axis=1).astype(jnp.bfloat16)
    grad_wqkv = jnp.dot(inputs.T, d_qkv, preferred_element_type=jnp.float32)
    input_term = jnp.dot(d_qkv, w_qkv.T, preferred_element_type=jnp.float32)
    return input_term, grad_wqkv, grad_wout


def reference(normed_input, segment_ids, weights_qkv, weights_out, cotangent):
    total = normed_input.shape[0]

    def visit(carry, index):
        acc_qkv, acc_out = carry
        cycle_pos = index // N_DP
        cycle = index % N_DP
        prev = (cycle_pos + N_BLK - 1) % N_BLK
        inputs = normed_input[index]
        grad_in = cotangent[index]
        seg_row = segment_ids[cycle, cycle_pos]
        term_a, gq_a, go_a = group_terms(inputs, seg_row, weights_qkv[cycle_pos], weights_out[cycle_pos], grad_in)
        term_b, gq_b, go_b = group_terms(inputs, seg_row, weights_qkv[prev], weights_out[prev], grad_in)
        acc_qkv = acc_qkv.at[cycle_pos].add(gq_a).at[prev].add(gq_b)
        acc_out = acc_out.at[cycle_pos].add(go_a).at[prev].add(go_b)
        return (acc_qkv, acc_out), (term_a + term_b).astype(jnp.bfloat16)

    start = (jnp.zeros(weights_qkv.shape, jnp.float32), jnp.zeros(weights_out.shape, jnp.float32))
    (acc_qkv, acc_out), input_grad = lax.scan(visit, start, jnp.arange(total, dtype=jnp.int32))
    return input_grad, acc_qkv.astype(jnp.bfloat16), acc_out.astype(jnp.bfloat16)
```

```python
import jax
import jax.numpy as jnp
from jax import lax
from jax.experimental import pallas as pl
from jax.experimental.pallas import tpu as pltpu
from jax.sharding import PartitionSpec as P

BF = jnp.bfloat16
F32 = jnp.float32
N_Z = 8


def dot(a, b, ca, cb):
    return lax.dot_general(a, b, (((ca,), (cb,)), ((), ())), preferred_element_type=F32)


def cost(flops, read):
    return pl.CostEstimate(flops=flops, bytes_accessed=read, transcendentals=0)


def params():
    return pltpu.CompilerParams(vmem_limit_bytes=32 * 1024 * 1024)


def attention_kernel(qkv_ref, datt_ref, seg_row_ref, seg_col_ref, dqkv_ref, att_ref):
    head = datt_ref.shape[1]
    count = datt_ref.shape[0]
    scale = head ** (-0.5)
    q = qkv_ref[:, :head]
    k = qkv_ref[:, head : 2 * head]
    v = qkv_ref[:, 2 * head :]
    datt = datt_ref[...]
    rows = lax.broadcasted_iota(jnp.int32, (count, count), 0)
    cols = lax.broadcasted_iota(jnp.int32, (count, count), 1)
    allowed = (rows >= cols) & (seg_col_ref[...] == seg_row_ref[...])
    scores = jnp.where(allowed, dot(q, k, 1, 1) * scale, F32(-1e30))
    top = jnp.max(scores, axis=-1, keepdims=True)
    expo = jnp.where(allowed, jnp.exp(scores - top), F32(0.0))
    probs = expo / jnp.sum(expo, axis=-1, keepdims=True)
    probs_b = probs.astype(BF)
    att_ref[...] = dot(probs_b, v, 1, 0).astype(BF)
    d_probs = dot(datt, v, 1, 1)
    inner = jnp.sum(probs * d_probs, axis=-1, keepdims=True)
    d_scores = (probs * (d_probs - inner) * scale).astype(BF)
    dqkv_ref[:, :head] = dot(d_scores, k, 1, 0).astype(BF)
    dqkv_ref[:, head : 2 * head] = dot(d_scores, q, 0, 0).astype(BF)
    dqkv_ref[:, 2 * head :] = dot(probs_b, datt, 0, 0).astype(BF)


def attention(qkv, datt, seg):
    count, head = datt.shape
    return pl.pallas_call(
        attention_kernel,
        out_shape=(
            jax.ShapeDtypeStruct((count, 3 * head), BF),
            jax.ShapeDtypeStruct((count, head), BF),
        ),
        compiler_params=params(),
        cost_estimate=cost(14 * count * count * head, 2 * count * head * 8),
        name="attention",
    )(qkv, datt, seg[None, :], seg[:, None])


def grads_kernel(x_ref, xf_ref, d_ref, df_ref, *outs):
    total = dot(x_ref[...], d_ref[...], 0, 0) + dot(xf_ref[...], df_ref[...], 0, 0)
    at = 0
    for out in outs:
        width = out.shape[1]
        out[...] = total[:, at : at + width].astype(BF)
        at += width


def grads(x, xf, d, df, widths, tile, name):
    count, model = x.shape
    whole = d.shape[1]
    step = pl.BlockSpec((count, tile), lambda i: (0, i))
    kept = pl.BlockSpec((count, whole), lambda i: (0, 0))
    return pl.pallas_call(
        grads_kernel,
        grid=(model // tile,),
        in_specs=[step, step, kept, kept],
        out_specs=[pl.BlockSpec((tile, w), lambda i: (i, 0)) for w in widths],
        out_shape=[jax.ShapeDtypeStruct((model, w), BF) for w in widths],
        compiler_params=params(),
        cost_estimate=cost(4 * count * model * whole, 4 * count * model + 2 * model * whole),
        name=name,
    )(x, xf, d, df)


def term_kernel(d_ref, w_ref, out_ref):
    out_ref[...] = dot(d_ref[...], w_ref[...], 1, 1).astype(BF)


def sum_term_kernel(d_ref, w_ref, far_ref, out_ref):
    out_ref[...] = (dot(d_ref[...], w_ref[...], 1, 1) + far_ref[...].astype(F32)).astype(BF)


def term(d, w, far=None, tile=1280):
    count, width = d.shape
    model = w.shape[0]
    specs = [
        pl.BlockSpec((count, width), lambda i: (0, 0)),
        pl.BlockSpec((tile, width), lambda i: (i, 0)),
    ]
    step = pl.BlockSpec((count, tile), lambda i: (0, i))
    return pl.pallas_call(
        term_kernel if far is None else sum_term_kernel,
        grid=(model // tile,),
        in_specs=specs + ([] if far is None else [step]),
        out_specs=step,
        out_shape=jax.ShapeDtypeStruct((count, model), BF),
        compiler_params=params(),
        cost_estimate=cost(2 * count * model * width, 2 * model * (width + 2 * count)),
        name="term" if far is None else "sum_term",
    )(d, w, *([] if far is None else [far]))


def shifted(block, distance):
    n = lax.axis_size("blk")
    return lax.ppermute(block, "blk", [(i, (i + distance) % n) for i in range(n)])


def z_shifted(block, distance):
    n = lax.axis_size("dp")
    route = [(i, i // N_Z * N_Z + (i + distance) % N_Z) for i in range(n)]
    return lax.ppermute(block, "dp", route)


def x_swapped(block):
    n = lax.axis_size("dp")
    return lax.ppermute(block, "dp", [(i, (i + N_Z) % n) for i in range(n)])


def z_reduced(parts):
    z = lax.axis_index("dp") % N_Z

    def at(distance):
        return lax.dynamic_index_in_dim(parts, (z + distance) % N_Z, 1, keepdims=False)

    across = at(4)
    up = z_shifted(across[0], 1)
    down = z_shifted(across[1], -1)
    third_up, third_down = at(3), at(-3)
    up = jnp.stack([third_up[0] + up, third_up[1]])
    down = jnp.stack([third_down[0], third_down[1] + down])
    up, down = z_shifted(up, 1), z_shifted(down, -1)
    up, down = z_shifted(at(2) + up, 1), z_shifted(at(-2) + down, -1)
    up, down = z_shifted(at(1) + up, 1), z_shifted(at(-1) + down, -1)
    return at(0).astype(F32) + up.astype(F32) + down.astype(F32)


def reduced_x_first(grad, x_hi):
    model, width = grad.shape
    halves = grad.reshape(2, model // 2, width)
    mine = lax.dynamic_index_in_dim(halves, x_hi, 0, keepdims=False)
    other = lax.dynamic_index_in_dim(halves, 1 - x_hi, 0, keepdims=False)
    mine = mine + x_swapped(other)
    rows = model // 2 // N_Z
    parts = mine.reshape(N_Z, 2, rows // 2, width).transpose(1, 0, 2, 3)
    return z_reduced(parts).reshape(rows, width).astype(BF)


def reduced_z_first(grad, x_hi):
    model, width = grad.shape
    rows = model // 2 // N_Z
    both = z_reduced(grad.reshape(2, N_Z, rows, width))
    mine = lax.dynamic_index_in_dim(both, x_hi, 0, keepdims=False)
    other = lax.dynamic_index_in_dim(both, 1 - x_hi, 0, keepdims=False)
    return (mine + x_swapped(other.astype(BF)).astype(F32)).astype(BF)


def local(normed_input, segment_ids, weights_qkv, weights_out, cotangent):
    x, wq, wo, g = normed_input[0], weights_qkv[0], weights_out[0], cotangent[0]
    n_blk = lax.axis_size("blk")
    here = lax.axis_index("blk")
    x_hi = lax.axis_index("dp") // N_Z
    head = wo.shape[0]
    seg = lax.dynamic_index_in_dim(segment_ids[0], here, 0, keepdims=False)
    seg_far = lax.dynamic_index_in_dim(segment_ids[0], (here + 1) % n_blk, 0, keepdims=False)

    x_far = shifted(x, -1)
    wo_back = shifted(wo, 1)
    qkv = jnp.dot(x, wq, preferred_element_type=F32).astype(BF)
    d_att = dot(g, wo, 1, 1).astype(BF)
    d_qkv, att = attention(qkv, d_att, seg)
    d_att_far = shifted(dot(g, wo_back, 1, 1).astype(BF), -1)
    g, x_far = lax.optimization_barrier((g, x_far))
    g_far = shifted(g, -1)

    qkv_far = jnp.dot(x_far, wq, preferred_element_type=F32).astype(BF)
    d_qkv_far, att_far = attention(qkv_far, d_att_far, seg_far)
    grad_qk, grad_v = grads(x, x_far, d_qkv, d_qkv_far, (2 * head, head), 1280, "grads_qkv")
    term_back = shifted(term(d_qkv_far, wq), 1)
    out_qk = reduced_x_first(grad_qk, x_hi)
    out_v = reduced_z_first(grad_v, x_hi)
    (grad_o,) = grads(g, g_far, att, att_far, (head,), 1280, "grads_out")
    out_o = reduced_z_first(grad_o, x_hi)
    input_grad = term(d_qkv, wq, term_back)
    return input_grad[None], jnp.concatenate([out_qk, out_v], axis=1)[None], out_o.T[None]


def solution(mesh):
    placed = (
        P(("blk", "dp"), None, None),
        P("dp", None, None),
        P("blk", None, None),
        P("blk", None, None),
        P(("blk", "dp"), None, None),
    )
    return jax.shard_map(
        local,
        mesh=mesh,
        in_specs=placed,
        out_specs=(P(("blk", "dp"), None, None), P("blk", "dp", None), P("blk", None, "dp")),
        check_vma=False,
    )
```

```python
import functools

import jax
import jax.numpy as jnp
from jax import lax
from jax.experimental import pallas as pl
from jax.experimental.pallas import tpu as pltpu
from jax.sharding import PartitionSpec as P

BF = jnp.bfloat16
F32 = jnp.float32
N_Z = 8


def dot(a, b, ca, cb):
    return lax.dot_general(a, b, (((ca,), (cb,)), ((), ())), preferred_element_type=F32)


def shape(dims, dtype=BF):
    return jax.ShapeDtypeStruct(dims, dtype)


def attention_of(qkv, datt, seg_row_ref, seg_col_ref, dqkv_ref, att_ref):
    count, head = datt.shape
    scale = head ** (-0.5)
    q = qkv[:, :head]
    k = qkv[:, head : 2 * head]
    v = qkv[:, 2 * head :]
    rows = lax.broadcasted_iota(jnp.int32, (count, count), 0)
    cols = lax.broadcasted_iota(jnp.int32, (count, count), 1)
    allowed = (rows >= cols) & (seg_col_ref[...] == seg_row_ref[...])
    scores = jnp.where(allowed, dot(q, k, 1, 1) * scale, F32(-1e30))
    top = jnp.max(scores, axis=-1, keepdims=True)
    expo = jnp.where(allowed, jnp.exp(scores - top), F32(0.0))
    probs = expo / jnp.sum(expo, axis=-1, keepdims=True)
    probs_b = probs.astype(BF)
    att_ref[...] = dot(probs_b, v, 1, 0).astype(BF)
    d_probs = dot(datt, v, 1, 1)
    inner = jnp.sum(probs * d_probs, axis=-1, keepdims=True)
    d_scores = (probs * (d_probs - inner) * scale).astype(BF)
    dqkv_ref[:, :head] = dot(d_scores, k, 1, 0).astype(BF)
    dqkv_ref[:, head : 2 * head] = dot(d_scores, q, 0, 0).astype(BF)
    dqkv_ref[:, 2 * head :] = dot(probs_b, datt, 0, 0).astype(BF)


def whole(kernel, name, limit, args, in_hbm, outs, scratch=(), flops=1):
    here = pl.BlockSpec(memory_space=pltpu.VMEM)
    there = pl.BlockSpec(memory_space=pltpu.HBM)
    return pl.pallas_call(
        kernel,
        in_specs=[here] * (len(args) - in_hbm) + [there] * in_hbm,
        out_specs=[here] * len(outs),
        out_shape=outs,
        scratch_shapes=scratch,
        compiler_params=pltpu.CompilerParams(vmem_limit_bytes=limit * 1024 * 1024),
        cost_estimate=pl.CostEstimate(flops=flops, bytes_accessed=1, transcendentals=0),
        name=name,
    )(*args)


def fetch_rows(n, src, dst, sem):
    tile = src.shape[0] // n
    return [
        pltpu.make_async_copy(
            src.at[pl.ds(i * tile, tile)], dst.at[pl.ds(i * tile, tile)], sem.at[i]
        )
        for i in range(n)
    ]


def projected(x_ref, w_ref, copies):
    tile = w_ref.shape[0] // len(copies)
    total = 0.0
    for i, copy in enumerate(copies):
        copy.wait()
        total += dot(x_ref[:, i * tile : (i + 1) * tile], w_ref[i * tile : (i + 1) * tile], 1, 0)
    return total.astype(BF)


def add_up(pairs, outs, tile):
    for start in range(0, pairs[0][0].shape[1], tile):
        total = sum(dot(x[:, start : start + tile], d, 0, 0) for x, d in pairs)
        column = 0
        for out in outs:
            width = out.shape[1]
            out[start : start + tile] = total[:, column : column + width].astype(BF)
            column += width


N_W = 4
TILE = 1280
SMALL, LARGE = 14, 48


def own_kernel(
    seg_row_ref, seg_col_ref, x_hbm, w_hbm, g_hbm, wo_hbm, dqkv_ref, att_ref,
    x_ref, w_ref, g_ref, wo_ref, w_sem, sems,
):
    x_copy = pltpu.make_async_copy(x_hbm, x_ref, sems.at[0])
    w_copies = fetch_rows(N_W, w_hbm, w_ref, w_sem)
    g_copy = pltpu.make_async_copy(g_hbm, g_ref, sems.at[1])
    wo_copy = pltpu.make_async_copy(wo_hbm, wo_ref, sems.at[2])
    for copy in (x_copy, *w_copies, g_copy, wo_copy):
        copy.start()
    x_copy.wait()
    qkv = projected(x_ref, w_ref, w_copies)
    g_copy.wait()
    wo_copy.wait()
    datt = dot(g_ref[...], wo_ref[...], 1, 1).astype(BF)
    attention_of(qkv, datt, seg_row_ref, seg_col_ref, dqkv_ref, att_ref)


def own_pair(x, w, g, wo, seg):
    count = x.shape[0]
    head = wo.shape[0]
    return whole(
        own_kernel,
        "own_pair",
        LARGE,
        (seg[None, :], seg[:, None], x, w, g, wo),
        4,
        [shape((count, 3 * head)), shape((count, head))],
        [pltpu.VMEM(a.shape, BF) for a in (x, w, g, wo)]
        + [pltpu.SemaphoreType.DMA((N_W,)), pltpu.SemaphoreType.DMA((3,))],
    )


def far_kernel(
    xf_ref, datt_ref, seg_row_ref, seg_col_ref, d_ref, w_hbm, x_hbm, dqkv_ref, att_ref, *rest
):
    outs, (w_ref, x_ref, w_sem, x_sem) = rest[:-4], rest[-4:]
    w_copies = fetch_rows(N_W, w_hbm, w_ref, w_sem)
    x_copy = pltpu.make_async_copy(x_hbm, x_ref, x_sem)
    for copy in (*w_copies, x_copy):
        copy.start()
    qkv = projected(xf_ref, w_ref, w_copies)
    attention_of(qkv, datt_ref[...], seg_row_ref, seg_col_ref, dqkv_ref, att_ref)
    x_copy.wait()
    add_up([(x_ref, d_ref[...]), (xf_ref, dqkv_ref[...])], outs, TILE)


def far_pair(x_far, datt, seg, d_own, w, x, widths):
    count, model = x.shape
    head = datt.shape[1]
    return whole(
        far_kernel,
        "far_pair",
        LARGE,
        (x_far, datt, seg[None, :], seg[:, None], d_own, w, x),
        2,
        [shape((count, 3 * head)), shape((count, head))] + [shape((model, n)) for n in widths],
        [pltpu.VMEM(w.shape, BF), pltpu.VMEM(x.shape, BF)]
        + [pltpu.SemaphoreType.DMA((N_W,)), pltpu.SemaphoreType.DMA],
    )


def grads_kernel(*refs):
    out_ref = refs[-1]
    pairs = [(refs[i], refs[i + 1][...]) for i in range(0, len(refs) - 1, 2)]
    add_up(pairs, [out_ref], TILE)


def grads_out(*pairs):
    out = shape((pairs[0][0].shape[1], pairs[0][1].shape[1]))
    args = [a for pair in pairs for a in pair]
    return whole(grads_kernel, "grads_out", SMALL, args, 0, [out])[0]


def first_pair(z):
    return (z + 3) // 2 % (N_Z // 2)


def columns_kernel(after_ref, g_hbm, near_ref, rest_ref, sems):
    z = lax.axis_index("dp") % N_Z
    model = g_hbm.shape[1]
    width = model // N_Z
    copies = []
    for i, out in enumerate((near_ref, rest_ref)):
        for x_hi in range(2):
            for k in range(2):
                pair = (first_pair(z) + 2 * i + k) % (N_Z // 2)
                start = pl.multiple_of(x_hi * (model // 2) + pair * width, 128)
                copies.append(
                    pltpu.make_async_copy(
                        g_hbm.at[:, pl.ds(start, width)],
                        out.at[:, pl.ds((2 * x_hi + k) * width, width)],
                        sems.at[len(copies)],
                    )
                )
    for copy in copies:
        copy.start()
    for copy in copies:
        copy.wait()


def columns_of(g, after):
    outs = [shape((g.shape[0], g.shape[1] // 2))] * 2
    return whole(
        columns_kernel, "columns", SMALL, (after, g), 1, outs, [pltpu.SemaphoreType.DMA((8,))]
    )


def term_kernel(d_ref, w_ref, *rest):
    out_ref = rest[-1]
    for start in range(0, w_ref.shape[0], TILE):
        total = dot(d_ref[...], w_ref[start : start + TILE], 1, 1)
        if len(rest) == 2:
            total += rest[0][:, start : start + TILE].astype(F32)
        out_ref[:, start : start + TILE] = total.astype(BF)


def term(d, w, *far):
    name = "sum_term" if far else "far_term"
    out = shape((d.shape[0], w.shape[0]))
    return whole(term_kernel, name, SMALL, (d, w, *far), 0, [out], (), 4 * d.shape[0] * w.size)[0]


def shifted(block, distance):
    n = lax.axis_size("blk")
    return lax.ppermute(block, "blk", [(i, (i + distance) % n) for i in range(n)])


def z_shifted(block, distance):
    n = lax.axis_size("dp")
    route = [(i, i // N_Z * N_Z + (i + distance) % N_Z) for i in range(n)]
    return lax.ppermute(block, "dp", route)


def x_swapped(block):
    n = lax.axis_size("dp")
    return lax.ppermute(block, "dp", [(i, (i + N_Z) % n) for i in range(n)])


def entry(part, distance):
    z = lax.axis_index("dp") % N_Z
    return lax.dynamic_index_in_dim(part, (z + distance) % N_Z, 1, keepdims=False)


def payload(at, step, moving):
    if step == 1:
        across = at(4)
        half = across.shape[1] // 2
        return across[:, :half], across[:, half:]
    up, down = moving
    if step == 2:
        half = up.shape[1]
        third_up, third_down = at(3), at(-3)
        up = jnp.concatenate([third_up[:, :half] + up, third_up[:, half:]], axis=1)
        down = jnp.concatenate([third_down[:, :half], third_down[:, half:] + down], axis=1)
        return up, down
    return at(5 - step) + up, at(step - 5) + down


def z_send(both):
    return z_shifted(both[0], 1), z_shifted(both[1], -1)


def z_end(at, moving):
    up, down = moving
    return at(0).astype(F32) + up.astype(F32) + down.astype(F32)


def halves_of(both, x_hi):
    mine = lax.dynamic_index_in_dim(both, x_hi, 0, keepdims=False)
    other = lax.dynamic_index_in_dim(both, 1 - x_hi, 0, keepdims=False)
    return mine, other


def x_end(both, x_hi):
    mine, other = halves_of(both, x_hi)
    return mine + x_swapped(other.astype(BF)).astype(F32)


def local(normed_input, segment_ids, weights_qkv, weights_out, cotangent):
    x, wq, wo, g = normed_input[0], weights_qkv[0], weights_out[0], cotangent[0]
    n_blk = lax.axis_size("blk")
    here = lax.axis_index("blk")
    x_hi = lax.axis_index("dp") // N_Z
    head = wo.shape[0]
    seg = lax.dynamic_index_in_dim(segment_ids[0], here, 0, keepdims=False)
    seg_far = lax.dynamic_index_in_dim(segment_ids[0], (here + 1) % n_blk, 0, keepdims=False)

    model = x.shape[1]
    half = model // 2
    rows = half // N_Z
    x_far = shifted(x, -1)
    wo_back = shifted(wo, 1)
    together = lax.optimization_barrier
    split = lambda grad: grad.reshape(2, N_Z, rows, grad.shape[1])
    d_qkv, att = own_pair(x, wq, g, wo, seg)
    wo_back, d_qkv = together((wo_back, d_qkv))
    d_att_home = dot(g, wo_back, 1, 1).astype(BF)
    d_att_far = shifted(d_att_home, -1)
    columns = columns_of(g, d_att_home)
    near, d_att_far = together((columns[0], d_att_far))
    columns_far = [shifted(near, -1), None]
    d_qkv_far, att_far, grad_qk, grad_v = far_pair(
        x_far, d_att_far, seg_far, d_qkv, wq, x, (2 * head, head)
    )

    rest_of, att_far = together((columns[1], att_far))
    columns_far[1] = shifted(rest_of, -1)
    grad_qk, grad_v = split(grad_qk), split(grad_v)
    first = functools.partial(entry, grad_qk)
    z = lax.axis_index("dp") % N_Z

    def terms_o(i):
        grad = grads_out((columns[i], att), (columns_far[i], att_far))
        return grad.reshape(2, N_Z // 2, rows, head)

    def second(distance):
        at = (z + distance - 2 * first_pair(z)) % N_Z
        grad_o = lax.dynamic_index_in_dim(terms, at, 1, keepdims=False)
        return jnp.concatenate([entry(grad_v, distance), grad_o], axis=2)

    sent = z_send(payload(first, 1, None))
    sent, columns_far[0] = together((sent, columns_far[0]))
    terms = near = terms_o(0)
    sent_2 = z_send(payload(second, 1, None))
    load, d_qkv_far = together((payload(first, 2, sent), d_qkv_far))
    sent = z_send(load)
    term_back = shifted(term(d_qkv_far, wq), 1)
    load, columns_far[1] = together((payload(second, 2, sent_2), columns_far[1]))
    sent_2 = z_send(load)
    terms = jnp.concatenate([near, terms_o(1)], axis=1)
    sent = z_send(payload(first, 3, sent))
    sent_2 = z_send(payload(second, 3, sent_2))
    load, term_back = together((payload(first, 4, sent), term_back))
    sent = z_send(load)
    sent_2 = z_send(payload(second, 4, sent_2))
    input_grad = term(d_qkv, wq, term_back)
    ends = jnp.concatenate([z_end(first, sent), z_end(second, sent_2)], axis=2)
    ends, input_grad = together((ends, input_grad))
    total = x_end(ends, x_hi).astype(BF)
    return input_grad[None], total[:, : 3 * head][None], total[:, 3 * head :].T[None]


def solution(mesh):
    placed = (
        P(("blk", "dp"), None, None),
        P("dp", None, None),
        P("blk", None, None),
        P("blk", None, None),
        P(("blk", "dp"), None, None),
    )
    return jax.shard_map(
        local,
        mesh=mesh,
        in_specs=placed,
        out_specs=(P(("blk", "dp"), None, None), P("blk", "dp", None), P("blk", None, "dp")),
        check_vma=False,
    )
```

```python
import functools

import jax
import jax.numpy as jnp
from jax import lax
from jax.experimental import pallas as pl
from jax.experimental.pallas import tpu as pltpu
from jax.sharding import PartitionSpec as P

BF = jnp.bfloat16
F32 = jnp.float32
N_Z = 8


def dot(a, b, ca, cb):
    return lax.dot_general(a, b, (((ca,), (cb,)), ((), ())), preferred_element_type=F32)


def shape(dims, dtype=BF):
    return jax.ShapeDtypeStruct(dims, dtype)


def attention_of(qkv, datt, seg_row_ref, seg_col_ref, dqkv_ref, att_ref):
    count, head = datt.shape
    scale = head ** (-0.5)
    q = qkv[:, :head]
    k = qkv[:, head : 2 * head]
    v = qkv[:, 2 * head :]
    rows = lax.broadcasted_iota(jnp.int32, (count, count), 0)
    cols = lax.broadcasted_iota(jnp.int32, (count, count), 1)
    allowed = (rows >= cols) & (seg_col_ref[...] == seg_row_ref[...])
    scores = jnp.where(allowed, dot(q, k, 1, 1) * scale, F32(-1e30))
    top = jnp.max(scores, axis=-1, keepdims=True)
    expo = jnp.where(allowed, jnp.exp(scores - top), F32(0.0))
    probs = expo / jnp.sum(expo, axis=-1, keepdims=True)
    probs_b = probs.astype(BF)
    att_ref[...] = dot(probs_b, v, 1, 0).astype(BF)
    d_probs = dot(datt, v, 1, 1)
    inner = jnp.sum(probs * d_probs, axis=-1, keepdims=True)
    d_scores = (probs * (d_probs - inner) * scale).astype(BF)
    dqkv_ref[:, :head] = dot(d_scores, k, 1, 0).astype(BF)
    dqkv_ref[:, head : 2 * head] = dot(d_scores, q, 0, 0).astype(BF)
    dqkv_ref[:, 2 * head :] = dot(probs_b, datt, 0, 0).astype(BF)


def whole(kernel, name, limit, args, in_hbm, outs, scratch=(), flops=1):
    here = pl.BlockSpec(memory_space=pltpu.VMEM)
    there = pl.BlockSpec(memory_space=pl.ANY)
    split = len(args) - in_hbm
    args = [*args[:split], *(pltpu.with_memory_space_constraint(a, pltpu.HBM) for a in args[split:])]
    return pl.pallas_call(
        kernel,
        in_specs=[here] * (len(args) - in_hbm) + [there] * in_hbm,
        out_specs=[here] * len(outs),
        out_shape=outs,
        scratch_shapes=scratch,
        compiler_params=pltpu.CompilerParams(vmem_limit_bytes=limit * 1024 * 1024),
        cost_estimate=pl.CostEstimate(flops=flops, bytes_accessed=1, transcendentals=0),
        name=name,
    )(*args)


def fetch_rows(n, src, dst, sem):
    tile = src.shape[0] // n
    return [
        pltpu.make_async_copy(
            src.at[pl.ds(i * tile, tile)], dst.at[pl.ds(i * tile, tile)], sem.at[i]
        )
        for i in range(n)
    ]


def projected(x_ref, w_ref, copies):
    tile = w_ref.shape[0] // len(copies)
    total = 0.0
    for i, copy in enumerate(copies):
        copy.wait()
        total += dot(x_ref[:, i * tile : (i + 1) * tile], w_ref[i * tile : (i + 1) * tile], 1, 0)
    return total.astype(BF)


def add_up(pairs, outs, tile):
    for start in range(0, pairs[0][0].shape[1], tile):
        total = sum(dot(x[:, start : start + tile], d, 0, 0) for x, d in pairs)
        column = 0
        for out in outs:
            width = out.shape[1]
            out[start : start + tile] = total[:, column : column + width].astype(BF)
            column += width


N_W = 4
TILE = 1280
SMALL, LARGE = 14, 20


def own_kernel(
    seg_row_ref, seg_col_ref, x_hbm, w_hbm, g_hbm, wo_hbm, dqkv_ref, att_ref,
    x_ref, w_ref, g_ref, wo_ref, w_sem, sems,
):
    x_copy = pltpu.make_async_copy(x_hbm, x_ref, sems.at[0])
    w_copies = fetch_rows(N_W, w_hbm, w_ref, w_sem)
    g_copy = pltpu.make_async_copy(g_hbm, g_ref, sems.at[1])
    wo_copy = pltpu.make_async_copy(wo_hbm, wo_ref, sems.at[2])
    for copy in (x_copy, *w_copies, g_copy, wo_copy):
        copy.start()
    x_copy.wait()
    qkv = projected(x_ref, w_ref, w_copies)
    g_copy.wait()
    wo_copy.wait()
    datt = dot(g_ref[...], wo_ref[...], 1, 1).astype(BF)
    attention_of(qkv, datt, seg_row_ref, seg_col_ref, dqkv_ref, att_ref)


def own_pair(x, w, g, wo, seg):
    count = x.shape[0]
    head = wo.shape[0]
    return whole(
        own_kernel,
        "own_pair",
        LARGE,
        (seg[None, :], seg[:, None], x, w, g, wo),
        4,
        [shape((count, 3 * head)), shape((count, head))],
        [pltpu.VMEM(a.shape, BF) for a in (x, w, g, wo)]
        + [pltpu.SemaphoreType.DMA((N_W,)), pltpu.SemaphoreType.DMA((3,))],
    )


def far_kernel(
    xf_ref, datt_ref, seg_row_ref, seg_col_ref, d_ref, w_hbm, x_hbm, dqkv_ref, att_ref, *rest
):
    outs, (w_ref, x_ref, w_sem, x_sem) = rest[:-4], rest[-4:]
    w_copies = fetch_rows(N_W, w_hbm, w_ref, w_sem)
    x_copy = pltpu.make_async_copy(x_hbm, x_ref, x_sem)
    for copy in (*w_copies, x_copy):
        copy.start()
    qkv = projected(xf_ref, w_ref, w_copies)
    attention_of(qkv, datt_ref[...], seg_row_ref, seg_col_ref, dqkv_ref, att_ref)
    x_copy.wait()
    add_up([(x_ref, d_ref[...]), (xf_ref, dqkv_ref[...])], outs, TILE)


def far_pair(x_far, datt, seg, d_own, w, x, widths):
    count, model = x.shape
    head = datt.shape[1]
    return whole(
        far_kernel,
        "far_pair",
        LARGE,
        (x_far, datt, seg[None, :], seg[:, None], d_own, w, x),
        2,
        [shape((count, 3 * head)), shape((count, head))] + [shape((model, n)) for n in widths],
        [pltpu.VMEM(w.shape, BF), pltpu.VMEM(x.shape, BF)]
        + [pltpu.SemaphoreType.DMA((N_W,)), pltpu.SemaphoreType.DMA],
    )


def grads_kernel(*refs):
    out_ref = refs[-1]
    pairs = [(refs[i], refs[i + 1][...]) for i in range(0, len(refs) - 1, 2)]
    add_up(pairs, [out_ref], TILE)


def grads_out(*pairs):
    out = shape((pairs[0][0].shape[1], pairs[0][1].shape[1]))
    args = [a for pair in pairs for a in pair]
    return whole(grads_kernel, "grads_out", SMALL, args, 0, [out])[0]


def first_pair(z):
    return (z + 3) // 2 % (N_Z // 2)


def columns_kernel(after_ref, g_hbm, near_ref, rest_ref, sems):
    z = lax.axis_index("dp") % N_Z
    model = g_hbm.shape[1]
    width = model // N_Z
    copies = []
    for i, out in enumerate((near_ref, rest_ref)):
        for x_hi in range(2):
            for k in range(2):
                pair = (first_pair(z) + 2 * i + k) % (N_Z // 2)
                start = pl.multiple_of(x_hi * (model // 2) + pair * width, 128)
                copies.append(
                    pltpu.make_async_copy(
                        g_hbm.at[:, pl.ds(start, width)],
                        out.at[:, pl.ds((2 * x_hi + k) * width, width)],
                        sems.at[len(copies)],
                    )
                )
    for copy in copies:
        copy.start()
    for copy in copies:
        copy.wait()


def columns_of(g, after):
    outs = [shape((g.shape[0], g.shape[1] // 2))] * 2
    return whole(
        columns_kernel, "columns", SMALL, (after, g), 1, outs, [pltpu.SemaphoreType.DMA((8,))]
    )


def term_kernel(d_ref, w_ref, out_ref):
    for start in range(0, w_ref.shape[0], TILE):
        total = dot(d_ref[...], w_ref[start : start + TILE], 1, 1)
        out_ref[:, start : start + TILE] = total.astype(BF)


def far_term(d, w):
    out = shape((d.shape[0], w.shape[0]))
    return whole(term_kernel, "far_term", SMALL, (d, w), 0, [out], (), 4 * d.shape[0] * w.size)[0]


def own_term_kernel(d_ref, w_hbm, out_hbm, w_ref, out_ref, w_sem, sem):
    w_copies = fetch_rows(N_W, w_hbm, w_ref, w_sem)
    for copy in w_copies:
        copy.start()
    tile = w_ref.shape[0] // N_W
    for i, copy in enumerate(w_copies):
        copy.wait()
        part = slice(i * tile, (i + 1) * tile)
        out_ref[:, part] = dot(d_ref[...], w_ref[part], 1, 1).astype(BF)
    out_copy = pltpu.make_async_copy(out_ref, out_hbm, sem)
    out_copy.start()
    out_copy.wait()


def own_term(d, w):
    dims = (d.shape[0], w.shape[0])
    return pl.pallas_call(
        own_term_kernel,
        in_specs=[pl.BlockSpec(memory_space=pltpu.VMEM), pl.BlockSpec(memory_space=pl.ANY)],
        out_specs=pl.BlockSpec(memory_space=pl.ANY),
        out_shape=pltpu.HBM(dims, BF),
        scratch_shapes=[
            pltpu.VMEM(w.shape, BF),
            pltpu.VMEM(dims, BF),
            pltpu.SemaphoreType.DMA((N_W,)),
            pltpu.SemaphoreType.DMA,
        ],
        compiler_params=pltpu.CompilerParams(vmem_limit_bytes=LARGE * 1024 * 1024),
        cost_estimate=pl.CostEstimate(flops=1, bytes_accessed=1, transcendentals=0),
        name="own_term",
    )(d, pltpu.with_memory_space_constraint(w, pltpu.HBM))


def sum_kernel(far_ref, own_hbm, out_hbm, own_ref, out_ref, in_sem, out_sem):
    count, model = own_ref.shape
    n = model // TILE
    parts = [(slice(None), pl.ds(i * TILE, TILE)) for i in range(n)]
    ins = [
        pltpu.make_async_copy(own_hbm.at[p], own_ref.at[p], in_sem.at[i]) for i, p in enumerate(parts)
    ]
    outs = [
        pltpu.make_async_copy(out_ref.at[p], out_hbm.at[p], out_sem.at[i]) for i, p in enumerate(parts)
    ]
    for copy in ins:
        copy.start()
    for i in range(n):
        ins[i].wait()
        part = slice(i * TILE, (i + 1) * TILE)
        total = own_ref[:, part].astype(F32) + far_ref[:, part].astype(F32)
        out_ref[:, part] = total.astype(BF)
        outs[i].start()
    for copy in outs:
        copy.wait()


def sum_of(own, far):
    steps = own.shape[1] // TILE
    return pl.pallas_call(
        sum_kernel,
        in_specs=[pl.BlockSpec(memory_space=pltpu.VMEM), pl.BlockSpec(memory_space=pl.ANY)],
        out_specs=pl.BlockSpec(memory_space=pl.ANY),
        out_shape=pltpu.HBM(own.shape, BF),
        scratch_shapes=[
            pltpu.VMEM(own.shape, BF),
            pltpu.VMEM(own.shape, BF),
            pltpu.SemaphoreType.DMA((steps,)),
            pltpu.SemaphoreType.DMA((steps,)),
        ],
        compiler_params=pltpu.CompilerParams(vmem_limit_bytes=SMALL * 1024 * 1024),
        cost_estimate=pl.CostEstimate(flops=2 * 10**9, bytes_accessed=1, transcendentals=0),
        name="sum_term",
    )(far, pltpu.with_memory_space_constraint(own, pltpu.HBM))


def shifted(block, distance):
    n = lax.axis_size("blk")
    return lax.ppermute(block, "blk", [(i, (i + distance) % n) for i in range(n)])


def z_shifted(block, distance):
    n = lax.axis_size("dp")
    route = [(i, i // N_Z * N_Z + (i + distance) % N_Z) for i in range(n)]
    return lax.ppermute(block, "dp", route)


def x_swapped(block):
    n = lax.axis_size("dp")
    return lax.ppermute(block, "dp", [(i, (i + N_Z) % n) for i in range(n)])


def entry(part, distance):
    z = lax.axis_index("dp") % N_Z
    return lax.dynamic_index_in_dim(part, (z + distance) % N_Z, 1, keepdims=False)


def payload(at, step, moving):
    if step == 1:
        across = at(4)
        half = across.shape[1] // 2
        return across[:, :half], across[:, half:]
    up, down = moving
    if step == 2:
        half = up.shape[1]
        third_up, third_down = at(3), at(-3)
        up = jnp.concatenate([third_up[:, :half] + up, third_up[:, half:]], axis=1)
        down = jnp.concatenate([third_down[:, :half], third_down[:, half:] + down], axis=1)
        return up, down
    return at(5 - step) + up, at(step - 5) + down


def z_send(both):
    return z_shifted(both[0], 1), z_shifted(both[1], -1)


def z_end(at, moving):
    up, down = moving
    return at(0).astype(F32) + up.astype(F32) + down.astype(F32)


def halves_of(both, x_hi):
    mine = lax.dynamic_index_in_dim(both, x_hi, 0, keepdims=False)
    other = lax.dynamic_index_in_dim(both, 1 - x_hi, 0, keepdims=False)
    return mine, other


def x_end(both, x_hi):
    mine, other = halves_of(both, x_hi)
    return mine + x_swapped(other.astype(BF)).astype(F32)


def local(normed_input, segment_ids, weights_qkv, weights_out, cotangent):
    x, wq, wo, g = normed_input[0], weights_qkv[0], weights_out[0], cotangent[0]
    n_blk = lax.axis_size("blk")
    here = lax.axis_index("blk")
    x_hi = lax.axis_index("dp") // N_Z
    head = wo.shape[0]
    seg = lax.dynamic_index_in_dim(segment_ids[0], here, 0, keepdims=False)
    seg_far = lax.dynamic_index_in_dim(segment_ids[0], (here + 1) % n_blk, 0, keepdims=False)

    model = x.shape[1]
    half = model // 2
    rows = half // N_Z
    x_far = shifted(x, -1)
    wo_back = shifted(wo, 1)
    together = lax.optimization_barrier
    split = lambda grad: grad.reshape(2, N_Z, rows, grad.shape[1])
    d_qkv, att = own_pair(x, wq, g, wo, seg)
    term_own = own_term(d_qkv, wq)
    wo_back, d_qkv, term_own = together((wo_back, d_qkv, term_own))
    d_att_home = dot(g, wo_back, 1, 1).astype(BF)
    d_att_far = shifted(d_att_home, -1)
    columns = columns_of(g, d_att_home)
    near, d_att_far = together((columns[0], d_att_far))
    columns_far = [shifted(near, -1), None]
    d_qkv_far, att_far, grad_qk, grad_v = far_pair(
        x_far, d_att_far, seg_far, d_qkv, wq, x, (2 * head, head)
    )

    rest_of, att_far = together((columns[1], att_far))
    columns_far[1] = shifted(rest_of, -1)
    grad_qk, grad_v = split(grad_qk), split(grad_v)
    first = functools.partial(entry, grad_qk)
    z = lax.axis_index("dp") % N_Z

    def terms_o(i):
        grad = grads_out((columns[i], att), (columns_far[i], att_far))
        return grad.reshape(2, N_Z // 2, rows, head)

    def second(distance):
        at = (z + distance - 2 * first_pair(z)) % N_Z
        grad_o = lax.dynamic_index_in_dim(terms, at, 1, keepdims=False)
        return jnp.concatenate([entry(grad_v, distance), grad_o], axis=2)

    sent = z_send(payload(first, 1, None))
    terms = near = terms_o(0)
    sent_2 = z_send(payload(second, 1, None))
    load, d_qkv_far = together((payload(first, 2, sent), d_qkv_far))
    sent = z_send(load)
    term_back = shifted(far_term(d_qkv_far, wq), 1)
    load, columns_far[1] = together((payload(second, 2, sent_2), columns_far[1]))
    sent_2 = z_send(load)
    terms = jnp.concatenate([near, terms_o(1)], axis=1)
    sent = z_send(payload(first, 3, sent))
    sent_2 = z_send(payload(second, 3, sent_2))
    load, term_back = together((payload(first, 4, sent), term_back))
    sent = z_send(load)
    sent_2 = z_send(payload(second, 4, sent_2))
    ends = jnp.concatenate([z_end(first, sent), z_end(second, sent_2)], axis=2)
    ends, input_grad = together((ends, sum_of(term_own, term_back)))
    total = x_end(ends, x_hi).astype(BF)
    return input_grad[None], total[:, : 3 * head][None], total[:, 3 * head :].T[None]


def solution(mesh):
    placed = (
        P(("blk", "dp"), None, None),
        P("dp", None, None),
        P("blk", None, None),
        P("blk", None, None),
        P(("blk", "dp"), None, None),
    )
    return jax.shard_map(
        local,
        mesh=mesh,
        in_specs=placed,
        out_specs=(P(("blk", "dp"), None, None), P("blk", "dp", None), P("blk", None, "dp")),
        check_vma=False,
    )
```

```python
import functools

import jax
import jax.numpy as jnp
from jax import lax
from jax.experimental import pallas as pl
from jax.experimental.pallas import tpu as pltpu
from jax.sharding import PartitionSpec as P

BF = jnp.bfloat16
F32 = jnp.float32
N_Z = 8


def dot(a, b, ca, cb):
    return lax.dot_general(a, b, (((ca,), (cb,)), ((), ())), preferred_element_type=F32)


def shape(dims, dtype=BF):
    return jax.ShapeDtypeStruct(dims, dtype)


def attention_of(qkv, datt, seg_row_ref, seg_col_ref, dqkv_ref, att_ref):
    count, head = datt.shape
    scale = head ** (-0.5)
    q = qkv[:, :head]
    k = qkv[:, head : 2 * head]
    v = qkv[:, 2 * head :]
    rows = lax.broadcasted_iota(jnp.int32, (count, count), 0)
    cols = lax.broadcasted_iota(jnp.int32, (count, count), 1)
    allowed = (rows >= cols) & (seg_col_ref[...] == seg_row_ref[...])
    scores = jnp.where(allowed, dot(q, k, 1, 1) * scale, F32(-1e30))
    top = jnp.max(scores, axis=-1, keepdims=True)
    expo = jnp.where(allowed, jnp.exp(scores - top), F32(0.0))
    probs = expo / jnp.sum(expo, axis=-1, keepdims=True)
    probs_b = probs.astype(BF)
    att_ref[...] = dot(probs_b, v, 1, 0).astype(BF)
    d_probs = dot(datt, v, 1, 1)
    inner = jnp.sum(probs * d_probs, axis=-1, keepdims=True)
    d_scores = (probs * (d_probs - inner) * scale).astype(BF)
    dqkv_ref[:, :head] = dot(d_scores, k, 1, 0).astype(BF)
    dqkv_ref[:, head : 2 * head] = dot(d_scores, q, 0, 0).astype(BF)
    dqkv_ref[:, 2 * head :] = dot(probs_b, datt, 0, 0).astype(BF)


def whole(kernel, name, limit, args, in_hbm, outs, scratch=(), flops=1):
    here = pl.BlockSpec(memory_space=pltpu.VMEM)
    there = pl.BlockSpec(memory_space=pl.ANY)
    split = len(args) - in_hbm
    args = [*args[:split], *(pltpu.with_memory_space_constraint(a, pltpu.HBM) for a in args[split:])]
    return pl.pallas_call(
        kernel,
        in_specs=[here] * (len(args) - in_hbm) + [there] * in_hbm,
        out_specs=[here] * len(outs),
        out_shape=outs,
        scratch_shapes=scratch,
        compiler_params=pltpu.CompilerParams(vmem_limit_bytes=limit * 1024 * 1024),
        cost_estimate=pl.CostEstimate(flops=flops, bytes_accessed=1, transcendentals=0),
        name=name,
    )(*args)


def fetch_rows(n, src, dst, sem):
    tile = src.shape[0] // n
    return [
        pltpu.make_async_copy(
            src.at[pl.ds(i * tile, tile)], dst.at[pl.ds(i * tile, tile)], sem.at[i]
        )
        for i in range(n)
    ]


def projected(x_ref, w_ref, copies):
    tile = w_ref.shape[0] // len(copies)
    total = 0.0
    for i, copy in enumerate(copies):
        copy.wait()
        total += dot(x_ref[:, i * tile : (i + 1) * tile], w_ref[i * tile : (i + 1) * tile], 1, 0)
    return total.astype(BF)


def add_up(pairs, outs, tile):
    for start in range(0, pairs[0][0].shape[1], tile):
        total = sum(dot(x[:, start : start + tile], d, 0, 0) for x, d in pairs)
        column = 0
        for out in outs:
            width = out.shape[1]
            out[start : start + tile] = total[:, column : column + width].astype(BF)
            column += width


N_W = 4
TILE = 1280
SMALL, LARGE = 14, 20


def own_kernel(
    seg_row_ref, seg_col_ref, x_hbm, w_hbm, g_hbm, wo_hbm, dqkv_ref, att_ref,
    x_ref, w_ref, g_ref, wo_ref, w_sem, sems,
):
    x_copy = pltpu.make_async_copy(x_hbm, x_ref, sems.at[0])
    w_copies = fetch_rows(N_W, w_hbm, w_ref, w_sem)
    g_copy = pltpu.make_async_copy(g_hbm, g_ref, sems.at[1])
    wo_copy = pltpu.make_async_copy(wo_hbm, wo_ref, sems.at[2])
    for copy in (x_copy, *w_copies, g_copy, wo_copy):
        copy.start()
    x_copy.wait()
    qkv = projected(x_ref, w_ref, w_copies)
    g_copy.wait()
    wo_copy.wait()
    datt = dot(g_ref[...], wo_ref[...], 1, 1).astype(BF)
    attention_of(qkv, datt, seg_row_ref, seg_col_ref, dqkv_ref, att_ref)


def own_pair(x, w, g, wo, seg):
    count = x.shape[0]
    head = wo.shape[0]
    return whole(
        own_kernel,
        "own_pair",
        LARGE,
        (seg[None, :], seg[:, None], x, w, g, wo),
        4,
        [shape((count, 3 * head)), shape((count, head))],
        [pltpu.VMEM(a.shape, BF) for a in (x, w, g, wo)]
        + [pltpu.SemaphoreType.DMA((N_W,)), pltpu.SemaphoreType.DMA((3,))],
    )


def far_kernel(
    xf_ref, datt_ref, seg_row_ref, seg_col_ref, d_ref, w_hbm, x_hbm, dqkv_ref, att_ref, *rest
):
    outs, (w_ref, x_ref, w_sem, x_sem) = rest[:-4], rest[-4:]
    w_copies = fetch_rows(N_W, w_hbm, w_ref, w_sem)
    x_copy = pltpu.make_async_copy(x_hbm, x_ref, x_sem)
    for copy in (*w_copies, x_copy):
        copy.start()
    qkv = projected(xf_ref, w_ref, w_copies)
    attention_of(qkv, datt_ref[...], seg_row_ref, seg_col_ref, dqkv_ref, att_ref)
    x_copy.wait()
    add_up([(x_ref, d_ref[...]), (xf_ref, dqkv_ref[...])], outs, TILE)


def far_pair(x_far, datt, seg, d_own, w, x, widths):
    count, model = x.shape
    head = datt.shape[1]
    return whole(
        far_kernel,
        "far_pair",
        LARGE,
        (x_far, datt, seg[None, :], seg[:, None], d_own, w, x),
        2,
        [shape((count, 3 * head)), shape((count, head))] + [shape((model, n)) for n in widths],
        [pltpu.VMEM(w.shape, BF), pltpu.VMEM(x.shape, BF)]
        + [pltpu.SemaphoreType.DMA((N_W,)), pltpu.SemaphoreType.DMA],
    )


def grads_kernel(g_ref, att_ref, own_ref, out_ref):
    for start in range(0, g_ref.shape[1], TILE):
        total = dot(g_ref[:, start : start + TILE], att_ref[...], 0, 0)
        total += own_ref[start : start + TILE].astype(F32)
        out_ref[start : start + TILE] = total.astype(BF)


def grads_out(g, att, own):
    return whole(grads_kernel, "grads_out", SMALL, (g, att, own), 0, [shape(own.shape)])[0]


def first_pair(z):
    return (z + 3) // 2 % (N_Z // 2)


def columns_kernel(
    after_ref, att_ref, g_hbm, near_ref, rest_ref, own_near_ref, own_rest_ref, sems
):
    z = lax.axis_index("dp") % N_Z
    model = g_hbm.shape[1]
    width = model // N_Z
    copies = []
    for i, out in enumerate((near_ref, rest_ref)):
        for x_hi in range(2):
            for k in range(2):
                pair = (first_pair(z) + 2 * i + k) % (N_Z // 2)
                start = pl.multiple_of(x_hi * (model // 2) + pair * width, 128)
                copies.append(
                    pltpu.make_async_copy(
                        g_hbm.at[:, pl.ds(start, width)],
                        out.at[:, pl.ds((2 * x_hi + k) * width, width)],
                        sems.at[len(copies)],
                    )
                )
    for copy in copies:
        copy.start()
    for out, own_ref, some in (
        (near_ref, own_near_ref, copies[:4]), (rest_ref, own_rest_ref, copies[4:])
    ):
        for copy in some:
            copy.wait()
        add_up([(out, att_ref[...])], [own_ref], TILE)


def columns_of(g, att, after):
    half = g.shape[1] // 2
    outs = [shape((g.shape[0], half))] * 2 + [shape((half, att.shape[1]))] * 2
    return whole(
        columns_kernel, "columns", SMALL, (after, att, g), 1, outs, [pltpu.SemaphoreType.DMA((8,))]
    )


def term_kernel(d_ref, w_ref, out_ref):
    for start in range(0, w_ref.shape[0], TILE):
        total = dot(d_ref[...], w_ref[start : start + TILE], 1, 1)
        out_ref[:, start : start + TILE] = total.astype(BF)


def far_term(d, w):
    out = shape((d.shape[0], w.shape[0]))
    return whole(term_kernel, "far_term", SMALL, (d, w), 0, [out], (), 4 * d.shape[0] * w.size)[0]


def own_term_kernel(d_ref, w_hbm, out_hbm, w_ref, out_ref, w_sem, sem):
    w_copies = fetch_rows(N_W, w_hbm, w_ref, w_sem)
    for copy in w_copies:
        copy.start()
    tile = w_ref.shape[0] // N_W
    for i, copy in enumerate(w_copies):
        copy.wait()
        part = slice(i * tile, (i + 1) * tile)
        out_ref[:, part] = dot(d_ref[...], w_ref[part], 1, 1).astype(BF)
    out_copy = pltpu.make_async_copy(out_ref, out_hbm, sem)
    out_copy.start()
    out_copy.wait()


def own_term(d, w):
    dims = (d.shape[0], w.shape[0])
    return pl.pallas_call(
        own_term_kernel,
        in_specs=[pl.BlockSpec(memory_space=pltpu.VMEM), pl.BlockSpec(memory_space=pl.ANY)],
        out_specs=pl.BlockSpec(memory_space=pl.ANY),
        out_shape=pltpu.HBM(dims, BF),
        scratch_shapes=[
            pltpu.VMEM(w.shape, BF),
            pltpu.VMEM(dims, BF),
            pltpu.SemaphoreType.DMA((N_W,)),
            pltpu.SemaphoreType.DMA,
        ],
        compiler_params=pltpu.CompilerParams(vmem_limit_bytes=LARGE * 1024 * 1024),
        cost_estimate=pl.CostEstimate(flops=1, bytes_accessed=1, transcendentals=0),
        name="own_term",
    )(d, pltpu.with_memory_space_constraint(w, pltpu.HBM))


def sum_kernel(far_ref, own_hbm, out_hbm, own_ref, out_ref, in_sem, out_sem):
    count, model = own_ref.shape
    n = model // TILE
    parts = [(slice(None), pl.ds(i * TILE, TILE)) for i in range(n)]
    ins = [
        pltpu.make_async_copy(own_hbm.at[p], own_ref.at[p], in_sem.at[i]) for i, p in enumerate(parts)
    ]
    outs = [
        pltpu.make_async_copy(out_ref.at[p], out_hbm.at[p], out_sem.at[i]) for i, p in enumerate(parts)
    ]
    for copy in ins:
        copy.start()
    for i in range(n):
        ins[i].wait()
        part = slice(i * TILE, (i + 1) * TILE)
        total = own_ref[:, part].astype(F32) + far_ref[:, part].astype(F32)
        out_ref[:, part] = total.astype(BF)
        outs[i].start()
    for copy in outs:
        copy.wait()


def sum_of(own, far):
    steps = own.shape[1] // TILE
    return pl.pallas_call(
        sum_kernel,
        in_specs=[pl.BlockSpec(memory_space=pltpu.VMEM), pl.BlockSpec(memory_space=pl.ANY)],
        out_specs=pl.BlockSpec(memory_space=pl.ANY),
        out_shape=pltpu.HBM(own.shape, BF),
        scratch_shapes=[
            pltpu.VMEM(own.shape, BF),
            pltpu.VMEM(own.shape, BF),
            pltpu.SemaphoreType.DMA((steps,)),
            pltpu.SemaphoreType.DMA((steps,)),
        ],
        compiler_params=pltpu.CompilerParams(vmem_limit_bytes=SMALL * 1024 * 1024),
        cost_estimate=pl.CostEstimate(flops=2 * 10**9, bytes_accessed=1, transcendentals=0),
        name="sum_term",
    )(far, pltpu.with_memory_space_constraint(own, pltpu.HBM))


def shifted(block, distance):
    n = lax.axis_size("blk")
    return lax.ppermute(block, "blk", [(i, (i + distance) % n) for i in range(n)])


def z_shifted(block, distance):
    n = lax.axis_size("dp")
    route = [(i, i // N_Z * N_Z + (i + distance) % N_Z) for i in range(n)]
    return lax.ppermute(block, "dp", route)


def x_swapped(block):
    n = lax.axis_size("dp")
    return lax.ppermute(block, "dp", [(i, (i + N_Z) % n) for i in range(n)])


def entry(part, distance):
    z = lax.axis_index("dp") % N_Z
    return lax.dynamic_index_in_dim(part, (z + distance) % N_Z, 1, keepdims=False)


def payload(at, step, moving):
    if step == 1:
        across = at(4)
        half = across.shape[1] // 2
        return across[:, :half], across[:, half:]
    up, down = moving
    if step == 2:
        half = up.shape[1]
        third_up, third_down = at(3), at(-3)
        up = jnp.concatenate([third_up[:, :half] + up, third_up[:, half:]], axis=1)
        down = jnp.concatenate([third_down[:, :half], third_down[:, half:] + down], axis=1)
        return up, down
    return at(5 - step) + up, at(step - 5) + down


def z_send(both):
    return z_shifted(both[0], 1), z_shifted(both[1], -1)


def z_end(at, moving):
    up, down = moving
    return at(0).astype(F32) + up.astype(F32) + down.astype(F32)


def halves_of(both, x_hi):
    mine = lax.dynamic_index_in_dim(both, x_hi, 0, keepdims=False)
    other = lax.dynamic_index_in_dim(both, 1 - x_hi, 0, keepdims=False)
    return mine, other


def x_end(both, x_hi):
    mine, other = halves_of(both, x_hi)
    return mine + x_swapped(other.astype(BF)).astype(F32)


def local(normed_input, segment_ids, weights_qkv, weights_out, cotangent):
    x, wq, wo, g = normed_input[0], weights_qkv[0], weights_out[0], cotangent[0]
    n_blk = lax.axis_size("blk")
    here = lax.axis_index("blk")
    x_hi = lax.axis_index("dp") // N_Z
    head = wo.shape[0]
    seg = lax.dynamic_index_in_dim(segment_ids[0], here, 0, keepdims=False)
    seg_far = lax.dynamic_index_in_dim(segment_ids[0], (here + 1) % n_blk, 0, keepdims=False)

    model = x.shape[1]
    half = model // 2
    rows = half // N_Z
    x_far = shifted(x, -1)
    wo_back = shifted(wo, 1)
    together = lax.optimization_barrier
    split = lambda grad: grad.reshape(2, N_Z, rows, grad.shape[1])
    d_qkv, att = own_pair(x, wq, g, wo, seg)
    term_own = own_term(d_qkv, wq)
    wo_back, d_qkv, term_own = together((wo_back, d_qkv, term_own))
    d_att_home = dot(g, wo_back, 1, 1).astype(BF)
    d_att_far = shifted(d_att_home, -1)
    columns = columns_of(g, att, d_att_home)
    near, d_att_far = together((columns[0], d_att_far))
    columns_far = [shifted(near, -1), None]
    d_qkv_far, att_far, grad_qk, grad_v = far_pair(
        x_far, d_att_far, seg_far, d_qkv, wq, x, (2 * head, head)
    )

    rest_of, att_far = together((columns[1], att_far))
    columns_far[1] = shifted(rest_of, -1)
    grad_qk, grad_v = split(grad_qk), split(grad_v)
    first = functools.partial(entry, grad_qk)
    z = lax.axis_index("dp") % N_Z

    def terms_o(i):
        grad = grads_out(columns_far[i], att_far, columns[2 + i])
        return grad.reshape(2, N_Z // 2, rows, head)

    def second(distance):
        at = (z + distance - 2 * first_pair(z)) % N_Z
        grad_o = lax.dynamic_index_in_dim(terms, at, 1, keepdims=False)
        return jnp.concatenate([entry(grad_v, distance), grad_o], axis=2)

    sent = z_send(payload(first, 1, None))
    terms = near = terms_o(0)
    sent_2 = z_send(payload(second, 1, None))
    load, d_qkv_far = together((payload(first, 2, sent), d_qkv_far))
    sent = z_send(load)
    term_back = shifted(far_term(d_qkv_far, wq), 1)
    load, columns_far[1] = together((payload(second, 2, sent_2), columns_far[1]))
    sent_2 = z_send(load)
    terms = jnp.concatenate([near, terms_o(1)], axis=1)
    sent = z_send(payload(first, 3, sent))
    sent_2 = z_send(payload(second, 3, sent_2))
    load, term_back = together((payload(first, 4, sent), term_back))
    sent = z_send(load)
    sent_2 = z_send(payload(second, 4, sent_2))
    ends = jnp.concatenate([z_end(first, sent), z_end(second, sent_2)], axis=2)
    ends, input_grad = together((ends, sum_of(term_own, term_back)))
    total = x_end(ends, x_hi).astype(BF)
    return input_grad[None], total[:, : 3 * head][None], total[:, 3 * head :].T[None]


def solution(mesh):
    placed = (
        P(("blk", "dp"), None, None),
        P("dp", None, None),
        P("blk", None, None),
        P("blk", None, None),
        P(("blk", "dp"), None, None),
    )
    return jax.shard_map(
        local,
        mesh=mesh,
        in_specs=placed,
        out_specs=(P(("blk", "dp"), None, None), P("blk", "dp", None), P("blk", None, "dp")),
        check_vma=False,
    )
```

```python
import functools

import jax
import jax.numpy as jnp
from jax import lax
from jax.experimental import pallas as pl
from jax.experimental.pallas import tpu as pltpu
from jax.sharding import PartitionSpec as P

BF = jnp.bfloat16
F32 = jnp.float32
N_Z = 8


def dot(a, b, ca, cb):
    return lax.dot_general(a, b, (((ca,), (cb,)), ((), ())), preferred_element_type=F32)


def shape(dims, dtype=BF):
    return jax.ShapeDtypeStruct(dims, dtype)


def attention_of(qkv, datt, seg_row_ref, seg_col_ref, dqkv_ref, att_ref):
    count, head = datt.shape
    scale = head ** (-0.5)
    q = qkv[:, :head]
    k = qkv[:, head : 2 * head]
    v = qkv[:, 2 * head :]
    rows = lax.broadcasted_iota(jnp.int32, (count, count), 0)
    cols = lax.broadcasted_iota(jnp.int32, (count, count), 1)
    allowed = (rows >= cols) & (seg_col_ref[...] == seg_row_ref[...])
    scores = jnp.where(allowed, dot(q, k, 1, 1) * scale, F32(-1e30))
    top = jnp.max(scores, axis=-1, keepdims=True)
    expo = jnp.where(allowed, jnp.exp(scores - top), F32(0.0))
    probs = expo / jnp.sum(expo, axis=-1, keepdims=True)
    probs_b = probs.astype(BF)
    att_ref[...] = dot(probs_b, v, 1, 0).astype(BF)
    d_probs = dot(datt, v, 1, 1)
    inner = jnp.sum(probs * d_probs, axis=-1, keepdims=True)
    d_scores = (probs * (d_probs - inner) * scale).astype(BF)
    dqkv_ref[:, :head] = dot(d_scores, k, 1, 0).astype(BF)
    dqkv_ref[:, head : 2 * head] = dot(d_scores, q, 0, 0).astype(BF)
    dqkv_ref[:, 2 * head :] = dot(probs_b, datt, 0, 0).astype(BF)


def whole(kernel, name, limit, args, in_hbm, outs, scratch=(), flops=1):
    here = pl.BlockSpec(memory_space=pltpu.VMEM)
    there = pl.BlockSpec(memory_space=pl.ANY)
    split = len(args) - in_hbm
    args = [*args[:split], *(pltpu.with_memory_space_constraint(a, pltpu.HBM) for a in args[split:])]
    return pl.pallas_call(
        kernel,
        in_specs=[here] * (len(args) - in_hbm) + [there] * in_hbm,
        out_specs=[here] * len(outs),
        out_shape=outs,
        scratch_shapes=scratch,
        compiler_params=pltpu.CompilerParams(vmem_limit_bytes=limit * 1024 * 1024),
        cost_estimate=pl.CostEstimate(flops=flops, bytes_accessed=1, transcendentals=0),
        name=name,
    )(*args)


def fetch_rows(n, src, dst, sem):
    tile = src.shape[0] // n
    return [
        pltpu.make_async_copy(
            src.at[pl.ds(i * tile, tile)], dst.at[pl.ds(i * tile, tile)], sem.at[i]
        )
        for i in range(n)
    ]


def projected(x_ref, w_ref, copies):
    tile = w_ref.shape[0] // len(copies)
    total = 0.0
    for i, copy in enumerate(copies):
        copy.wait()
        total += dot(x_ref[:, i * tile : (i + 1) * tile], w_ref[i * tile : (i + 1) * tile], 1, 0)
    return total.astype(BF)


def add_up(pairs, outs, tile):
    for start in range(0, pairs[0][0].shape[1], tile):
        total = sum(dot(x[:, start : start + tile], d, 0, 0) for x, d in pairs)
        column = 0
        for out in outs:
            width = out.shape[1]
            out[start : start + tile] = total[:, column : column + width].astype(BF)
            column += width


N_W = 4
TILE = 2560
SMALL, LARGE = 14, 20


def own_kernel(
    seg_row_ref, seg_col_ref, x_hbm, w_hbm, g_hbm, wo_hbm, dqkv_ref, att_ref,
    x_ref, w_ref, g_ref, wo_ref, w_sem, sems,
):
    x_copy = pltpu.make_async_copy(x_hbm, x_ref, sems.at[0])
    w_copies = fetch_rows(N_W, w_hbm, w_ref, w_sem)
    g_copy = pltpu.make_async_copy(g_hbm, g_ref, sems.at[1])
    wo_copy = pltpu.make_async_copy(wo_hbm, wo_ref, sems.at[2])
    for copy in (x_copy, *w_copies, g_copy, wo_copy):
        copy.start()
    x_copy.wait()
    qkv = projected(x_ref, w_ref, w_copies)
    g_copy.wait()
    wo_copy.wait()
    datt = dot(g_ref[...], wo_ref[...], 1, 1).astype(BF)
    attention_of(qkv, datt, seg_row_ref, seg_col_ref, dqkv_ref, att_ref)


def own_pair(x, w, g, wo, seg):
    count = x.shape[0]
    head = wo.shape[0]
    return whole(
        own_kernel,
        "own_pair",
        LARGE,
        (seg[None, :], seg[:, None], x, w, g, wo),
        4,
        [shape((count, 3 * head)), shape((count, head))],
        [pltpu.VMEM(a.shape, BF) for a in (x, w, g, wo)]
        + [pltpu.SemaphoreType.DMA((N_W,)), pltpu.SemaphoreType.DMA((3,))],
    )


def far_kernel(
    xf_ref, datt_ref, seg_row_ref, seg_col_ref, d_ref, w_hbm, x_hbm, dqkv_ref, att_ref, *rest
):
    outs, (w_ref, x_ref, w_sem, x_sem) = rest[:-4], rest[-4:]
    w_copies = fetch_rows(N_W, w_hbm, w_ref, w_sem)
    x_copy = pltpu.make_async_copy(x_hbm, x_ref, x_sem)
    for copy in (*w_copies, x_copy):
        copy.start()
    qkv = projected(xf_ref, w_ref, w_copies)
    attention_of(qkv, datt_ref[...], seg_row_ref, seg_col_ref, dqkv_ref, att_ref)
    x_copy.wait()
    add_up([(x_ref, d_ref[...]), (xf_ref, dqkv_ref[...])], outs, TILE)


def far_pair(x_far, datt, seg, d_own, w, x, widths):
    count, model = x.shape
    head = datt.shape[1]
    return whole(
        far_kernel,
        "far_pair",
        LARGE,
        (x_far, datt, seg[None, :], seg[:, None], d_own, w, x),
        2,
        [shape((count, 3 * head)), shape((count, head))] + [shape((model, n)) for n in widths],
        [pltpu.VMEM(w.shape, BF), pltpu.VMEM(x.shape, BF)]
        + [pltpu.SemaphoreType.DMA((N_W,)), pltpu.SemaphoreType.DMA],
    )


def grads_kernel(g_ref, att_ref, own_ref, out_ref):
    for start in range(0, g_ref.shape[1], TILE):
        total = dot(g_ref[:, start : start + TILE], att_ref[...], 0, 0)
        total += own_ref[start : start + TILE].astype(F32)
        out_ref[start : start + TILE] = total.astype(BF)


def grads_out(g, att, own):
    return whole(grads_kernel, "grads_out", SMALL, (g, att, own), 0, [shape(own.shape)])[0]


def first_pair(z):
    return (z + 3) // 2 % (N_Z // 2)


def columns_kernel(
    after_ref, att_ref, g_hbm, near_ref, rest_ref, own_near_ref, own_rest_ref, sems
):
    z = lax.axis_index("dp") % N_Z
    model = g_hbm.shape[1]
    width = model // N_Z
    copies = []
    for i, out in enumerate((near_ref, rest_ref)):
        for x_hi in range(2):
            for k in range(2):
                pair = (first_pair(z) + 2 * i + k) % (N_Z // 2)
                start = pl.multiple_of(x_hi * (model // 2) + pair * width, 128)
                copies.append(
                    pltpu.make_async_copy(
                        g_hbm.at[:, pl.ds(start, width)],
                        out.at[:, pl.ds((2 * x_hi + k) * width, width)],
                        sems.at[len(copies)],
                    )
                )
    for copy in copies:
        copy.start()
    for out, own_ref, some in (
        (near_ref, own_near_ref, copies[:4]), (rest_ref, own_rest_ref, copies[4:])
    ):
        for copy in some:
            copy.wait()
        add_up([(out, att_ref[...])], [own_ref], TILE)


def columns_of(g, att, after):
    half = g.shape[1] // 2
    outs = [shape((g.shape[0], half))] * 2 + [shape((half, att.shape[1]))] * 2
    return whole(
        columns_kernel, "columns", SMALL, (after, att, g), 1, outs, [pltpu.SemaphoreType.DMA((8,))]
    )


def term_kernel(d_ref, w_ref, out_ref):
    for start in range(0, w_ref.shape[0], TILE):
        total = dot(d_ref[...], w_ref[start : start + TILE], 1, 1)
        out_ref[:, start : start + TILE] = total.astype(BF)


def far_term(d, w):
    out = shape((d.shape[0], w.shape[0]))
    return whole(term_kernel, "far_term", SMALL, (d, w), 0, [out], (), 4 * d.shape[0] * w.size)[0]


def own_term_kernel(d_ref, w_hbm, out_hbm, w_ref, out_ref, w_sem, sem):
    w_copies = fetch_rows(N_W, w_hbm, w_ref, w_sem)
    for copy in w_copies:
        copy.start()
    tile = w_ref.shape[0] // N_W
    for i, copy in enumerate(w_copies):
        copy.wait()
        part = slice(i * tile, (i + 1) * tile)
        out_ref[:, part] = dot(d_ref[...], w_ref[part], 1, 1).astype(BF)
    out_copy = pltpu.make_async_copy(out_ref, out_hbm, sem)
    out_copy.start()
    out_copy.wait()


def own_term(d, w):
    dims = (d.shape[0], w.shape[0])
    return pl.pallas_call(
        own_term_kernel,
        in_specs=[pl.BlockSpec(memory_space=pltpu.VMEM), pl.BlockSpec(memory_space=pl.ANY)],
        out_specs=pl.BlockSpec(memory_space=pl.ANY),
        out_shape=pltpu.HBM(dims, BF),
        scratch_shapes=[
            pltpu.VMEM(w.shape, BF),
            pltpu.VMEM(dims, BF),
            pltpu.SemaphoreType.DMA((N_W,)),
            pltpu.SemaphoreType.DMA,
        ],
        compiler_params=pltpu.CompilerParams(vmem_limit_bytes=LARGE * 1024 * 1024),
        cost_estimate=pl.CostEstimate(flops=1, bytes_accessed=1, transcendentals=0),
        name="own_term",
    )(d, pltpu.with_memory_space_constraint(w, pltpu.HBM))


def sum_kernel(far_ref, own_hbm, out_hbm, own_ref, out_ref, in_sem, out_sem):
    count, model = own_ref.shape
    n = model // TILE
    parts = [(slice(None), pl.ds(i * TILE, TILE)) for i in range(n)]
    ins = [
        pltpu.make_async_copy(own_hbm.at[p], own_ref.at[p], in_sem.at[i]) for i, p in enumerate(parts)
    ]
    outs = [
        pltpu.make_async_copy(out_ref.at[p], out_hbm.at[p], out_sem.at[i]) for i, p in enumerate(parts)
    ]
    for copy in ins:
        copy.start()
    for i in range(n):
        ins[i].wait()
        part = slice(i * TILE, (i + 1) * TILE)
        total = own_ref[:, part].astype(F32) + far_ref[:, part].astype(F32)
        out_ref[:, part] = total.astype(BF)
        outs[i].start()
    for copy in outs:
        copy.wait()


def sum_of(own, far):
    steps = own.shape[1] // TILE
    return pl.pallas_call(
        sum_kernel,
        in_specs=[pl.BlockSpec(memory_space=pltpu.VMEM), pl.BlockSpec(memory_space=pl.ANY)],
        out_specs=pl.BlockSpec(memory_space=pl.ANY),
        out_shape=pltpu.HBM(own.shape, BF),
        scratch_shapes=[
            pltpu.VMEM(own.shape, BF),
            pltpu.VMEM(own.shape, BF),
            pltpu.SemaphoreType.DMA((steps,)),
            pltpu.SemaphoreType.DMA((steps,)),
        ],
        compiler_params=pltpu.CompilerParams(vmem_limit_bytes=SMALL * 1024 * 1024),
        cost_estimate=pl.CostEstimate(flops=2 * 10**9, bytes_accessed=1, transcendentals=0),
        name="sum_term",
    )(far, pltpu.with_memory_space_constraint(own, pltpu.HBM))


def shifted(block, distance):
    n = lax.axis_size("blk")
    return lax.ppermute(block, "blk", [(i, (i + distance) % n) for i in range(n)])


def z_shifted(block, distance):
    n = lax.axis_size("dp")
    route = [(i, i // N_Z * N_Z + (i + distance) % N_Z) for i in range(n)]
    return lax.ppermute(block, "dp", route)


def x_swapped(block):
    n = lax.axis_size("dp")
    return lax.ppermute(block, "dp", [(i, (i + N_Z) % n) for i in range(n)])


def entry(part, distance):
    z = lax.axis_index("dp") % N_Z
    return lax.dynamic_index_in_dim(part, (z + distance) % N_Z, 1, keepdims=False)


def payload(at, step, moving):
    if step == 1:
        across = at(4)
        half = across.shape[1] // 2
        return across[:, :half], across[:, half:]
    up, down = moving
    if step == 2:
        half = up.shape[1]
        third_up, third_down = at(3), at(-3)
        up = jnp.concatenate([third_up[:, :half] + up, third_up[:, half:]], axis=1)
        down = jnp.concatenate([third_down[:, :half], third_down[:, half:] + down], axis=1)
        return up, down
    return at(5 - step) + up, at(step - 5) + down


def z_send(both):
    return z_shifted(both[0], 1), z_shifted(both[1], -1)


def z_end(at, moving):
    up, down = moving
    return at(0).astype(F32) + up.astype(F32) + down.astype(F32)


def halves_of(both, x_hi):
    mine = lax.dynamic_index_in_dim(both, x_hi, 0, keepdims=False)
    other = lax.dynamic_index_in_dim(both, 1 - x_hi, 0, keepdims=False)
    return mine, other


def x_end(both, x_hi):
    mine, other = halves_of(both, x_hi)
    return mine + x_swapped(other.astype(BF)).astype(F32)


def local(normed_input, segment_ids, weights_qkv, weights_out, cotangent):
    x, wq, wo, g = normed_input[0], weights_qkv[0], weights_out[0], cotangent[0]
    n_blk = lax.axis_size("blk")
    here = lax.axis_index("blk")
    x_hi = lax.axis_index("dp") // N_Z
    head = wo.shape[0]
    seg = lax.dynamic_index_in_dim(segment_ids[0], here, 0, keepdims=False)
    seg_far = lax.dynamic_index_in_dim(segment_ids[0], (here + 1) % n_blk, 0, keepdims=False)

    model = x.shape[1]
    half = model // 2
    rows = half // N_Z
    x_far = shifted(x, -1)
    wo_back = shifted(wo, 1)
    together = lax.optimization_barrier
    split = lambda grad: grad.reshape(2, N_Z, rows, grad.shape[1])
    d_qkv, att = own_pair(x, wq, g, wo, seg)
    term_own = own_term(d_qkv, wq)
    wo_back, d_qkv, term_own = together((wo_back, d_qkv, term_own))
    d_att_home = dot(g, wo_back, 1, 1).astype(BF)
    d_att_far = shifted(d_att_home, -1)
    columns = columns_of(g, att, d_att_home)
    near, d_att_far = together((columns[0], d_att_far))
    columns_far = [shifted(near, -1), None]
    d_qkv_far, att_far, grad_qk, grad_v = far_pair(
        x_far, d_att_far, seg_far, d_qkv, wq, x, (2 * head, head)
    )

    rest_of, att_far = together((columns[1], att_far))
    columns_far[1] = shifted(rest_of, -1)
    grad_qk, grad_v = split(grad_qk), split(grad_v)
    first = functools.partial(entry, grad_qk)
    z = lax.axis_index("dp") % N_Z

    def terms_o(i):
        grad = grads_out(columns_far[i], att_far, columns[2 + i])
        return grad.reshape(2, N_Z // 2, rows, head)

    def second(distance):
        at = (z + distance - 2 * first_pair(z)) % N_Z
        grad_o = lax.dynamic_index_in_dim(terms, at, 1, keepdims=False)
        return jnp.concatenate([entry(grad_v, distance), grad_o], axis=2)

    sent = z_send(payload(first, 1, None))
    terms = near = terms_o(0)
    sent_2 = z_send(payload(second, 1, None))
    load, d_qkv_far = together((payload(first, 2, sent), d_qkv_far))
    sent = z_send(load)
    term_back = shifted(far_term(d_qkv_far, wq), 1)
    load, columns_far[1] = together((payload(second, 2, sent_2), columns_far[1]))
    sent_2 = z_send(load)
    terms = jnp.concatenate([near, terms_o(1)], axis=1)
    sent = z_send(payload(first, 3, sent))
    sent_2 = z_send(payload(second, 3, sent_2))
    load, term_back = together((payload(first, 4, sent), term_back))
    sent = z_send(load)
    sent_2 = z_send(payload(second, 4, sent_2))
    ends = jnp.concatenate([z_end(first, sent), z_end(second, sent_2)], axis=2)
    ends, input_grad = together((ends, sum_of(term_own, term_back)))
    total = x_end(ends, x_hi).astype(BF)
    return input_grad[None], total[:, : 3 * head][None], total[:, 3 * head :].T[None]


def solution(mesh):
    placed = (
        P(("blk", "dp"), None, None),
        P("dp", None, None),
        P("blk", None, None),
        P("blk", None, None),
        P(("blk", "dp"), None, None),
    )
    return jax.shard_map(
        local,
        mesh=mesh,
        in_specs=placed,
        out_specs=(P(("blk", "dp"), None, None), P("blk", "dp", None), P("blk", None, "dp")),
        check_vma=False,
    )
```
